256 devices in a mesh: blk: 4 (over x_lo, core), wide: 64 (over y, x_hi, z).
Axes of the slice: x: 4 (x_hi: 2, x_lo: 2; x = x_hi * 2 + x_lo), y: 4, z: 8, core: 2. Of those that a mesh axis runs over, the one named last changes fastest.
Arguments:
- src_emb: float32 [4096, 1024], P('blk')
- src_sharp: float32 [4096], P('blk')
- tgt_emb: float32 [262144, 1024], P(('blk', 'wide'))
- tgt_sharp: float32 [262144], P(('blk', 'wide')), may hold values from 4 to 256
- cand_src: int32 [2048, 128], P(('blk', 'wide')), may hold values from 0 to 4095
- cand_tgt: int32 [2048, 128], P(('blk', 'wide')), may hold values from 0 to 127
- cand_count: int32 [2048], P(('blk', 'wide')), may hold values from 1 to 128, as said below
Outputs:
- margins: float32 [2048, 128], P(('blk', 'wide'))
The draws below stay inside these ranges and needn't reach their ends.
Inputs may be any that keep to these rules, and one draw needn't show every extreme that they name: `cand_count`: some tile uses all 128 slots in every draw.
All inputs are finite; a program needn't handle non-finite values.
Results may differ from the reference program's by a relative error of at most 0.0003.
Values sent between devices are 32-bit elements; how exact they have to be, the bound alone decides.
A program may use at most 128 MiB of HBM per device.

```python
import math
import jax
import jax.numpy as jnp
from jax import lax

D = 1024
TILE = 128
NEIGH = 16
S = 4096
TG = 262144
NT = 2048


def cluster_total():
    return max(8, min(256, S // 16))


def shared_labels(key):
    count = cluster_total()
    first_pick = jax.random.randint(jax.random.fold_in(key, 101), (S,), 0, count, jnp.int32)
    second_pick = jax.random.randint(jax.random.fold_in(key, 102), (S,), 0, count, jnp.int32)
    cluster_of = jnp.minimum(first_pick, second_pick)
    partner = jax.random.randint(jax.random.fold_in(key, 103), (TG,), 0, S, jnp.int32)
    return (cluster_of, partner)


def source_rows(key, mix_lo, mix_hi):
    cluster_of, partner = shared_labels(key)
    inverse = 1.0 / math.sqrt(D)
    centers = jax.random.normal(jax.random.fold_in(key, 104), (cluster_total(), D), jnp.float32) * inverse
    noise = jax.random.normal(jax.random.fold_in(key, 105), (S, D), jnp.float32) * inverse
    levels = jax.random.uniform(jax.random.fold_in(key, 106), (S, 1), jnp.float32)
    mixing = mix_lo + (mix_hi - mix_lo) * levels
    rows = mixing * centers[cluster_of] + jnp.sqrt(1.0 - mixing * mixing) * noise
    return (rows, cluster_of, partner, centers)


def slot_targets(key):
    return jax.random.randint(jax.random.fold_in(key, 111), (NT, TILE), 0, TILE, jnp.int32)


def draw_src_emb(key, part):
    rows, cluster_of, partner, centers = source_rows(key, 0.3, 0.9)
    return rows


def draw_tgt_emb(key, part):
    src_rows, cluster_of, partner, centers = source_rows(key, 0.3, 0.9)
    key = jax.random.fold_in(key, 2)
    inverse = 1.0 / math.sqrt(D)
    levels = jax.random.uniform(jax.random.fold_in(key, 6), (TG, 1), jnp.float32)
    tie_rate = 0.2 + 0.7 * levels
    other = jax.random.normal(jax.random.fold_in(key, 7), (TG, D), jnp.float32) * inverse
    backing = 0.6 * centers[cluster_of[partner]] + 0.8 * other
    rows = tie_rate * src_rows[partner] + jnp.sqrt(1.0 - tie_rate * tie_rate) * backing
    return rows


def draw_src_sharp(key, part):
    key = jax.random.fold_in(key, 3)
    levels = jax.random.uniform(key, (S,), jnp.float32)
    values = jnp.exp(jnp.log(4.0) + levels * jnp.log(64.0))
    return values


def draw_cand_count(key, part):
    key = jax.random.fold_in(key, 4)
    counts = jax.random.randint(key, (NT,), 1, TILE + 1, jnp.int32)
    return counts.at[::8].set(TILE)


def draw_cand_tgt(key, part):
    targets = slot_targets(key)
    return targets


def draw_cand_src(key, part):
    cluster_of, partner = shared_labels(key)
    targets = slot_targets(key)
    key = jax.random.fold_in(key, 13)
    random_src = jax.random.randint(jax.random.fold_in(key, 1), (NT, TILE), 0, S, jnp.int32)
    use_link = jax.random.randint(jax.random.fold_in(key, 2), (NT, TILE), 0, 2, jnp.int32)
    target_ids = jnp.arange(NT, dtype=jnp.int32)[:, None] * TILE + targets
    linked = partner[target_ids]
    return jnp.where(use_link == 1, linked, random_src)


def shard_levels(rng, dims, pieces, least, top_value):
    level, own = 1.0, jax.random.fold_in(rng, 6)
    for dim, blocks in pieces:
        heights = jnp.exp(jax.random.uniform(jax.random.fold_in(own, dim), (blocks,), jnp.float32, least / len(pieces), top_value / len(pieces)))
        level = level * jnp.repeat(heights, dims[dim] // blocks).reshape([-1 if axis == dim else 1 for axis in range(len(dims))])
    return level


def setup_inputs(seed: int = 0) -> dict:
    keys = jax.random.split(jax.random.key(seed), 8)
    return {
        "src_emb": draw_src_emb(jax.random.fold_in(keys[7], 71), 0),
        "src_sharp": draw_src_sharp(jax.random.fold_in(keys[7], 71), 0),
        "tgt_emb": draw_tgt_emb(jax.random.fold_in(keys[7], 71), 0),
        "tgt_sharp": jnp.clip(jnp.exp(math.log(256.0) - 4.158883 * jax.random.uniform(keys[3], (TG,), jnp.float32) ** shard_levels(keys[3], (TG,), ((0, 256),), -0.2, 0.2)), 4.0, 256.0),
        "cand_src": draw_cand_src(jax.random.fold_in(keys[7], 71), 0),
        "cand_tgt": draw_cand_tgt(jax.random.fold_in(keys[7], 71), 0),
        "cand_count": draw_cand_count(jax.random.fold_in(keys[7], 71), 0),
    }


def normalize(rows):
    return rows / jnp.sqrt(lax.optimization_barrier(jnp.sum(rows * rows, axis=1, keepdims=True)) + 1e-06)

def reference(src_emb, src_sharp, tgt_emb, tgt_sharp, cand_src, cand_tgt, cand_count):
    src_unit = normalize(src_emb)
    tgt_unit = normalize(tgt_emb)
    tgt_blocks = tgt_unit.reshape(-1, 4096, D)
    sharp_blocks = tgt_sharp.reshape(-1, 4096)

    def step(carry, item):
        fmax, fsum = carry
        rows, sharp_t = item
        cosine = jnp.dot(rows, src_unit.T, precision=lax.Precision.HIGHEST)
        back = sharp_t[:, None] * cosine
        back_max = lax.optimization_barrier(jnp.max(back, axis=1))
        bwd = (back_max + jnp.log(lax.optimization_barrier(jnp.sum(jnp.exp(back - back_max[:, None]), axis=1))) - jnp.log(jnp.float32(NEIGH))) / sharp_t
        ahead = src_sharp[None, :] * cosine
        newmax = jnp.maximum(fmax, lax.optimization_barrier(jnp.max(ahead, axis=0)))
        fsum = fsum * jnp.exp(fmax - newmax) + lax.optimization_barrier(jnp.sum(jnp.exp(ahead - newmax[None, :]), axis=0))
        return ((newmax, fsum), bwd)
    init = (jnp.full((S,), -1e+30, jnp.float32), jnp.zeros((S,), jnp.float32))
    (fmax, fsum), bwd = lax.scan(step, init, (tgt_blocks, sharp_blocks))
    bwd = bwd.reshape(TG)
    fwd = (fmax + jnp.log(fsum) - jnp.log(jnp.float32(NEIGH))) / src_sharp
    tile_ids = jnp.arange(NT, dtype=jnp.int32).reshape(-1, 32)
    groups = (cand_src.reshape(-1, 32, TILE), cand_tgt.reshape(-1, 32, TILE), cand_count.reshape(-1, 32), tile_ids)

    def score(item):
        sources, targets, counts, tiles = item
        target_ids = tiles[:, None] * TILE + targets
        pair = lax.optimization_barrier(jnp.sum(src_unit[sources] * tgt_unit[target_ids], axis=-1))
        denom = jnp.maximum(0.5 * (fwd[sources] + bwd[target_ids]), 0.5)
        valid = jnp.arange(TILE, dtype=jnp.int32)[None, :] < counts[:, None]
        return jnp.where(valid, pair / denom, 0.0)
    return lax.map(score, groups).reshape(NT, TILE)
```

```python
import jax
import jax.numpy as jnp
from jax import lax
from jax.experimental import pallas as pl
from jax.experimental.pallas import tpu as pltpu
from jax.sharding import PartitionSpec as P

LOG2E = 1.4426950408889634
LN2 = 0.6931471805599453
MESH = pl.DeviceIdType.MESH
D = 1024
ROWS = 1024
UNIT = 128
HALF = 512
SUB = 64
ROUNDS = 4
NTILE = 256
RELAY_STEP = (6, 12, 17, 23)
MATE_STEP = (12, 17, 23, 28)


def log2(v):
    return jnp.log(v) * LOG2E


def combine(parts):
    top = jnp.max(parts, axis=0)
    return top + log2(jnp.sum(jnp.exp2(parts - top[None]), axis=0))


def kernel(
    src_hbm, sharp_in, tgt_hbm, tsharp_ref, cand_smem, cand_ref, ctgt_ref, count_ref, out_ref,
    srcall, cos, tgt_raw, t_hi, t_lo, s_hi, s_lo, sharp_all, lse, part_a, part_b, fwd_all,
    top_y, sum_y, bwd8, picked, pair8,
    load_sem, own_send, own_recv, x_send, x_recv, y_send, y_recv, mx_send, mx_recv, my_send, my_recv,
    sh_send, sh_recv, a_send, a_recv, b_send, b_recv, c_send, c_recv,
):
    b = lax.axis_index("blk")
    w = lax.axis_index("wide")
    x_lo, core = b // 2, b % 2
    y, x_hi, z = w // 16, (w // 8) % 2, w % 8
    x = x_hi * 2 + x_lo
    par = y % 2
    opp = 1 - x_lo
    mate_b = x_lo * 2 + 1 - core
    opp_b = opp * 2 + core
    opp_mate_b = opp * 2 + 1 - core

    def at(xx, yy):
        return ((xx % 2) * 2 + core, yy * 16 + (xx // 2) * 8 + z)

    right, left = at((x + 1) % 4, y), at((x + 3) % 4, y)
    up, down = at(x, (y + 1) % 4), at(x, (y + 3) % 4)
    mate = (mate_b, w)
    me_a = core * 8 + z
    me_b = x_lo * 8 + w // 8

    def peer_a(d):
        a = (me_a + d) % 16
        return (x_lo * 2 + a // 8, (w // 8) * 8 + a % 8)

    def peer_b(d):
        g = (me_b + d) % 16
        return ((g // 8) * 2 + core, (g % 8) * 8 + z)

    own_base = b * ROWS
    first = par * HALF
    second = (1 - par) * HALF

    def load_src(i, offset):
        return pltpu.make_async_copy(
            src_hbm.at[pl.ds(offset, HALF)],
            srcall.at[pl.ds(pl.multiple_of(own_base + offset, HALF), HALF)],
            load_sem.at[i],
        )

    loads = [load_src(0, first), load_src(1, second)]
    load_tgt = pltpu.make_async_copy(tgt_hbm, tgt_raw, load_sem.at[2])
    for load in loads:
        load.start()
    load_tgt.start()

    barrier = pltpu.get_barrier_semaphore()

    def greet(d, _):
        pl.semaphore_signal(barrier, inc=1, device_id=peer_a(d), device_id_type=MESH)
        pl.semaphore_signal(barrier, inc=1, device_id=peer_b(d), device_id_type=MESH)
        return 0

    lax.fori_loop(1, 16, greet, 0)
    pl.semaphore_signal(barrier, inc=1, device_id=(opp_mate_b, w), device_id_type=MESH)

    def unit_rows(ref, start):
        def body(i, _):
            at_rows = pl.ds(pl.multiple_of(start + i * 32, 32), 32)
            rows = ref[at_rows, :]
            norm = jnp.sum(rows * rows, axis=1, keepdims=True) + 1e-06
            ref[at_rows, :] = rows / jnp.sqrt(norm)
            return 0

        lax.fori_loop(0, HALF // 32, body, 0)

    loads[0].wait()
    unit_rows(srcall, own_base + first)
    pl.semaphore_wait(barrier, 31)

    def remote(rows, count, send, recv, where):
        there = srcall.at[pl.ds(pl.multiple_of(rows, SUB), count)]
        return pltpu.make_async_remote_copy(
            src_ref=there, dst_ref=there, send_sem=send, recv_sem=recv,
            device_id=where, device_id_type=MESH,
        )

    def x_copies(k):
        at_row = own_base + first + k * UNIT
        return (
            remote(at_row, SUB, x_send.at[k, 0], x_recv.at[k, 0], right),
            remote(at_row + SUB, SUB, x_send.at[k, 1], x_recv.at[k, 1], left),
        )

    def x_arrivals(k):
        at_row = opp_b * ROWS + first + k * UNIT
        return (
            remote(at_row, SUB, x_send.at[k, 0], x_recv.at[k, 0], right),
            remote(at_row + SUB, SUB, x_send.at[k, 1], x_recv.at[k, 1], left),
        )

    def y_copies(k):
        at_row = opp_b * ROWS + first + k * UNIT
        return (
            remote(at_row, SUB, y_send.at[k, 0], y_recv.at[k, 0], up),
            remote(at_row + SUB, SUB, y_send.at[k, 1], y_recv.at[k, 1], down),
        )

    def y_arrivals(k):
        at_row = opp_b * ROWS + second + k * UNIT
        return (
            remote(at_row, SUB, y_send.at[k, 0], y_recv.at[k, 0], up),
            remote(at_row + SUB, SUB, y_send.at[k, 1], y_recv.at[k, 1], down),
        )

    def mx_copy(k, block):
        return remote(block * ROWS + first + k * UNIT, UNIT, mx_send.at[k], mx_recv.at[k], mate)

    def my_copy(k, block):
        return remote(block * ROWS + second + k * UNIT, UNIT, my_send.at[k], my_recv.at[k], mate)

    def own_copy(i, block):
        return remote(block * ROWS + (first, second)[i], HALF, own_send.at[i], own_recv.at[i], mate)

    def sharp_copy(i, block, where):
        there = sharp_all.at[pl.ds(block * 8, 8)]
        return pltpu.make_async_remote_copy(
            src_ref=there, dst_ref=there, send_sem=sh_send.at[i], recv_sem=sh_recv.at[i],
            device_id=where, device_id_type=MESH,
        )

    for k in range(ROUNDS):
        for copy in x_copies(k):
            copy.start()
    sharp_all[pl.ds(b * 8, 8)] = sharp_in[...]
    sharp_to = ((mate_b, w), (opp_b, w), (opp_mate_b, w))
    for i, where in enumerate(sharp_to):
        sharp_copy(i, b, where).start()
    own_copy(0, b).start()
    loads[1].wait()
    unit_rows(srcall, own_base + second)
    own_copy(1, b).start()

    load_tgt.wait()

    def split_target(t):
        rows = tgt_raw[t * 128:(t + 1) * 128, :]
        norm = jnp.sum(rows * rows, axis=1, keepdims=True) + 1e-06
        turned = (rows / jnp.sqrt(norm)).T
        high = turned.astype(jnp.bfloat16)
        t_hi[:, t * 128:(t + 1) * 128] = high
        t_lo[:, t * 128:(t + 1) * 128] = (turned - high.astype(jnp.float32)).astype(jnp.bfloat16)

    for t in range(8):
        split_target(t)
    top_y[...] = jnp.full(top_y.shape, -1e30, jnp.float32)
    sum_y[...] = jnp.zeros(sum_y.shape, jnp.float32)
    for i, block in enumerate((mate_b, opp_b, opp_mate_b)):
        sharp_copy(i, block, sharp_to[i]).wait_recv()

    eye = lax.broadcasted_iota(jnp.int32, (128, 128), 0) == lax.broadcasted_iota(jnp.int32, (128, 128), 1)

    def unit_of(j, i):
        block = jnp.where(j < 2, b, mate_b)
        near = block * 8 + (j % 2) * 4 + i
        far_block = opp_b if i < 2 else opp_mate_b
        far = far_block * 8 + (par if i % 2 == 0 else 1 - par) * 4 + (j - 4)
        return jnp.where(j < 4, near, far)

    def step(s, _):
        j = s // 4
        n = s % 4
        for k in range(ROUNDS):
            @pl.when(s == RELAY_STEP[k])
            def _(k=k):
                for copy in x_arrivals(k):
                    copy.wait_recv()
                for copy in y_copies(k):
                    copy.start()
                mx_copy(k, opp_b).start()

            @pl.when(s == MATE_STEP[k])
            def _(k=k):
                for copy in y_arrivals(k):
                    copy.wait_recv()
                my_copy(k, opp_b).start()

            @pl.when(s == 16 + 4 * k)
            def _(k=k):
                mx_copy(k, opp_mate_b).wait_recv()
                my_copy(k, opp_mate_b).wait_recv()

        @pl.when(s == 8)
        def _():
            for i in range(2):
                own_copy(i, mate_b).wait_recv()

        @pl.when(n == 0)
        def _():
            for i in range(4):
                rows = srcall[pl.ds(pl.multiple_of(unit_of(j, i) * UNIT, UNIT), UNIT), :]
                high = rows.astype(jnp.bfloat16)
                s_hi[i * UNIT:(i + 1) * UNIT, :] = high
                s_lo[i * UNIT:(i + 1) * UNIT, :] = (rows - high.astype(jnp.float32)).astype(jnp.bfloat16)

        at_n = pl.ds(pl.multiple_of(n * NTILE, NTILE), NTILE)
        high_t, low_t = t_hi[:, at_n], t_lo[:, at_n]
        tile = jnp.dot(s_hi[...], high_t, preferred_element_type=jnp.float32)
        tile += jnp.dot(s_hi[...], low_t, preferred_element_type=jnp.float32)
        tile += jnp.dot(s_lo[...], high_t, preferred_element_type=jnp.float32)
        for i in range(4):
            at_unit = pl.ds(pl.multiple_of(unit_of(j, i) * UNIT, UNIT), UNIT)
            for part in range(NTILE // 128):
                cos[n * (NTILE // 128) + part, at_unit, :] = tile[i * UNIT:(i + 1) * UNIT, part * 128:(part + 1) * 128]
        scale = tsharp_ref[:, at_n] * LOG2E
        old = top_y[:, at_n]
        new = jnp.maximum(old, scale * jnp.max(tile, axis=0, keepdims=True))
        mass = jnp.sum(jnp.exp2(tile * scale - new), axis=0, keepdims=True)
        sum_y[:, at_n] = sum_y[:, at_n] * jnp.exp2(old - new) + mass
        top_y[:, at_n] = new

        @pl.when(n == 3)
        def _():
            for i in range(4):
                unit = unit_of(j, i)
                ahead = cos[:, pl.ds(pl.multiple_of(unit * UNIT, UNIT), UNIT), :]
                row = jnp.broadcast_to(sharp_all[unit] * LOG2E, (128, 128))
                column = jnp.sum(jnp.where(eye, row, 0.0), axis=1, keepdims=True)
                ahead = ahead * column[None]
                peak = jnp.max(jnp.max(ahead, axis=0), axis=1, keepdims=True)
                total = peak + log2(jnp.sum(jnp.sum(jnp.exp2(ahead - peak[None]), axis=0), axis=1, keepdims=True))
                lse[unit] = jnp.sum(jnp.where(eye, jnp.broadcast_to(total, (128, 128)), 0.0), axis=0, keepdims=True)

        return 0

    lax.fori_loop(0, 32, step, 0)

    def to_a(d):
        owner = (me_a + d) % 16
        return pltpu.make_async_remote_copy(
            src_ref=lse.at[pl.ds(owner * 2, 2)], dst_ref=part_a.at[d - 1], send_sem=a_send, recv_sem=a_recv,
            device_id=peer_a(d), device_id_type=MESH,
        )

    def start_a(d, _):
        to_a(d).start()
        return 0

    lax.fori_loop(1, 16, start_a, 0)

    def pick(t):
        def body(i, _):
            for u in range(16):
                slot = i * 16 + u
                picked[pl.ds(slot, 1), :] = cos[t, pl.ds(cand_smem[t, slot], 1), :]
            return 0

        lax.fori_loop(0, 8, body, 0)
        want = lax.broadcasted_iota(jnp.int32, (128, 128), 0) == ctgt_ref[t:t + 1, :]
        pair8[t:t + 1, :] = jnp.sum(jnp.where(want, picked[...].T, 0.0), axis=0, keepdims=True)

    for t in range(4):
        pick(t)
    pltpu.make_async_copy(part_a, part_a, a_recv).wait()
    mine = lse[pl.ds(me_a * 2, 2)]
    part_b[0] = combine(jnp.concatenate([part_a[...], mine[None]], axis=0))

    def start_b(d, _):
        pltpu.make_async_remote_copy(
            src_ref=part_b.at[0], dst_ref=part_b.at[d], send_sem=b_send, recv_sem=b_recv,
            device_id=peer_b(d), device_id_type=MESH,
        ).start()
        return 0

    lax.fori_loop(1, 16, start_b, 0)
    for t in range(4, 8):
        pick(t)
    scale_y = tsharp_ref[...]
    bwd = (top_y[...] + log2(sum_y[...]) - 4.0) * LN2 / scale_y
    for t in range(8):
        bwd8[t:t + 1, :] = bwd[:, t * 128:(t + 1) * 128]
    pltpu.make_async_copy(part_b.at[pl.ds(1, 15)], part_b.at[pl.ds(1, 15)], b_recv).wait()
    fwd_all[me_a] = (combine(part_b[...]) - 4.0) * LN2 / sharp_all[pl.ds(me_a * 2, 2)]

    def start_c(d, _):
        there = fwd_all.at[me_a]
        pltpu.make_async_remote_copy(
            src_ref=there, dst_ref=there, send_sem=c_send, recv_sem=c_recv,
            device_id=peer_a(d), device_id_type=MESH,
        ).start()
        return 0

    lax.fori_loop(1, 16, start_c, 0)

    for k in range(ROUNDS):
        for copy in (*x_copies(k), *y_copies(k)):
            copy.wait_send()
        mx_copy(k, opp_b).wait_send()
        my_copy(k, opp_b).wait_send()
    for i in range(2):
        own_copy(i, b).wait_send()
    for i, where in enumerate(sharp_to):
        sharp_copy(i, b, where).wait_send()
    pltpu.make_async_copy(part_a, part_a, a_send).wait()
    pltpu.make_async_copy(part_b.at[pl.ds(1, 15)], part_b.at[pl.ds(1, 15)], b_send).wait()

    def lookup(table, index):
        return jnp.take_along_axis(table, index, axis=1, mode="promise_in_bounds")

    bwd_cand = lookup(bwd8[...], ctgt_ref[...])
    sources = cand_ref[...]
    low, high = sources % 128, sources // 128
    counts = jnp.zeros((8, 128), jnp.int32)
    tile_id = lax.broadcasted_iota(jnp.int32, (8, 128), 0)
    for t in range(8):
        counts = jnp.where(tile_id == t, count_ref[t], counts)
    valid = lax.broadcasted_iota(jnp.int32, (8, 128), 1) < counts

    pltpu.make_async_copy(part_a, part_a, c_recv).wait()
    pltpu.make_async_copy(part_a, part_a, c_send).wait()
    fwd_cand = jnp.zeros((8, 128), jnp.float32)
    for r in range(32):
        row = jnp.broadcast_to(fwd_all[r // 2, r % 2], (8, 128))
        fwd_cand = jnp.where(high == r, lookup(row, low), fwd_cand)
    denom = jnp.maximum(0.5 * (fwd_cand + bwd_cand), 0.5)
    out_ref[...] = jnp.where(valid, pair8[...] / denom, 0.0)


def per_device(src_emb, src_sharp, tgt_emb, tgt_sharp, cand_src, cand_tgt, cand_count):
    vmem = pl.BlockSpec(memory_space=pltpu.VMEM)
    smem = pl.BlockSpec(memory_space=pltpu.SMEM)
    hbm = pl.BlockSpec(memory_space=pl.ANY)
    dma = pltpu.SemaphoreType.DMA
    f32, bf16 = jnp.float32, jnp.bfloat16
    return pl.pallas_call(
        kernel,
        out_shape=jax.ShapeDtypeStruct((8, 128), f32),
        in_specs=[hbm, vmem, hbm, vmem, smem, vmem, vmem, smem],
        out_specs=vmem,
        scratch_shapes=[
            pltpu.VMEM((4 * ROWS, D), f32),
            pltpu.VMEM((8, 4 * ROWS, 128), f32),
            pltpu.VMEM((ROWS, D), f32),
            pltpu.VMEM((D, ROWS), bf16),
            pltpu.VMEM((D, ROWS), bf16),
            pltpu.VMEM((HALF, D), bf16),
            pltpu.VMEM((HALF, D), bf16),
            pltpu.VMEM((32, 1, 128), f32),
            pltpu.VMEM((32, 1, 128), f32),
            pltpu.VMEM((15, 2, 1, 128), f32),
            pltpu.VMEM((16, 2, 1, 128), f32),
            pltpu.VMEM((16, 2, 1, 128), f32),
            pltpu.VMEM((1, ROWS), f32),
            pltpu.VMEM((1, ROWS), f32),
            pltpu.VMEM((8, 128), f32),
            pltpu.VMEM((128, 128), f32),
            pltpu.VMEM((8, 128), f32),
            dma((3,)), dma((2,)), dma((2,)), dma((4, 2)), dma((4, 2)), dma((4, 2)), dma((4, 2)),
            dma((4,)), dma((4,)), dma((4,)), dma((4,)), dma((3,)), dma((3,)),
            dma, dma, dma, dma, dma, dma,
        ],
        compiler_params=pltpu.CompilerParams(
            collective_id=0, has_side_effects=True, vmem_limit_bytes=60 * 1024 * 1024
        ),
        cost_estimate=pl.CostEstimate(flops=6 * 4096 * 1024 * 1024, bytes_accessed=8 << 20, transcendentals=8 << 20),
    )(
        src_emb, src_sharp.reshape(8, 1, 128), tgt_emb, tgt_sharp.reshape(1, ROWS),
        cand_src, cand_src, cand_tgt, cand_count,
    )


def solution(mesh):
    placed = (
        P("blk", None),
        P("blk"),
        P(("blk", "wide"), None),
        P(("blk", "wide")),
        P(("blk", "wide"), None),
        P(("blk", "wide"), None),
        P(("blk", "wide")),
    )
    return jax.shard_map(
        per_device, mesh=mesh, in_specs=placed, out_specs=P(("blk", "wide"), None), check_vma=False
    )
```

```python
import jax
import jax.numpy as jnp
from jax import lax
from jax.experimental import pallas as pl
from jax.experimental.pallas import tpu as pltpu
from jax.sharding import PartitionSpec as P

LOG2E = 1.4426950408889634
LN2 = 0.6931471805599453
MESH = pl.DeviceIdType.MESH
D = 1024
ROWS = 1024
UNIT = 128
HALF = 512
QUARTER = 256
PIECE = 32
X_SLOT = (-1, 2, 4, 5)
RELAY_SLOT = (5, 7, 9, 10)
CROSS_SLOT = (12, 15)
MATE_SLOT = (17, 20)
ROUND_SLOT = (12, 15, 18, 21)


def log2(v):
    return jnp.log(v) * LOG2E


def combine(parts):
    top = jnp.max(parts, axis=0)
    return top + log2(jnp.sum(jnp.exp2(parts - top[None]), axis=0))


def kernel(
    src_hbm, sharp_in, tgt_hbm, tsharp_ref, cand_smem, cand_ref, ctgt_ref, count_ref, out_ref,
    srcall, cos, tgt_raw, t_hi, t_lo, s_hi, s_lo, sharp_all, lse, part_a, part_b, fwd_all,
    buf_a, buf_b, scale_x, peak_x, top_y, sum_y, bwd8, picked, pair8,
    load_sem, own_send, own_recv, x_send, x_recv, y_send, y_recv, z_send, z_recv,
    dy_send, dy_recv, dz_send, dz_recv, m_send, m_recv,
    sh_send, sh_recv, a_send, a_recv, b_send, b_recv, c_send, c_recv,
):
    b = lax.axis_index("blk")
    w = lax.axis_index("wide")
    x_lo, core = b // 2, b % 2
    y, x_hi, z = w // 16, (w // 8) % 2, w % 8
    x = x_hi * 2 + x_lo
    row_q, col_q = y % 2, z % 2
    q_x = row_q * 2 + col_q
    q_y = (1 - row_q) * 2 + col_q
    q_z = row_q * 2 + 1 - col_q
    q_d = (1 - row_q) * 2 + 1 - col_q
    opp = 1 - x_lo
    mate_b = x_lo * 2 + 1 - core
    opp_b = opp * 2 + core
    opp_mate_b = opp * 2 + 1 - core

    def at(xx, yy, zz):
        return ((xx % 2) * 2 + core, yy * 16 + (xx // 2) * 8 + zz)

    x_next, x_prev = at((x + 1) % 4, y, z), at((x + 3) % 4, y, z)
    y_next, y_prev = at(x, (y + 1) % 4, z), at(x, (y + 3) % 4, z)
    z_next, z_prev = at(x, y, (z + 1) % 8), at(x, y, (z + 7) % 8)
    mate = (mate_b, w)
    me_a = core * 8 + z
    me_b = x_lo * 8 + w // 8

    def peer_a(d):
        a = (me_a + d) % 16
        return (x_lo * 2 + a // 8, (w // 8) * 8 + a % 8)

    def peer_b(d):
        g = (me_b + d) % 16
        return ((g // 8) * 2 + core, (g % 8) * 8 + z)

    own_base = b * ROWS

    def load_src(i):
        return pltpu.make_async_copy(
            src_hbm.at[pl.ds(i * HALF, HALF)],
            srcall.at[pl.ds(pl.multiple_of(own_base + i * HALF, HALF), HALF)],
            load_sem.at[i],
        )

    loads = [load_src(0), load_src(1)]
    load_tgt = pltpu.make_async_copy(tgt_hbm, tgt_raw, load_sem.at[2])
    for load in loads:
        load.start()
    load_tgt.start()

    barrier = pltpu.get_barrier_semaphore()

    def greet(d, _):
        pl.semaphore_signal(barrier, inc=1, device_id=peer_a(d), device_id_type=MESH)
        pl.semaphore_signal(barrier, inc=1, device_id=peer_b(d), device_id_type=MESH)
        return 0

    lax.fori_loop(1, 16, greet, 0)
    pl.semaphore_signal(barrier, inc=1, device_id=(opp_mate_b, w), device_id_type=MESH)

    def unit_rows(ref, start):
        def body(i, _):
            at_rows = pl.ds(pl.multiple_of(start + i * 32, 32), 32)
            rows = ref[at_rows, :]
            norm = jnp.sum(rows * rows, axis=1, keepdims=True) + 1e-06
            ref[at_rows, :] = rows / jnp.sqrt(norm)
            return 0

        lax.fori_loop(0, HALF // 32, body, 0)

    def remote(rows, count, send, recv, where):
        there = srcall.at[pl.ds(pl.multiple_of(rows, PIECE), count)]
        return pltpu.make_async_remote_copy(
            src_ref=there, dst_ref=there, send_sem=send, recv_sem=recv,
            device_id=where, device_id_type=MESH,
        )

    def piece(block, quarter, k, side):
        return block * ROWS + quarter * QUARTER + (k // 2) * UNIT + side * 64 + (k % 2) * PIECE

    def both(block, quarter, k, send, recv, where):
        return tuple(
            remote(piece(block, quarter, k, side), PIECE, send.at[k, side], recv.at[k, side], where[side])
            for side in range(2)
        )

    along_x, along_y, along_z = (x_next, x_prev), (y_next, y_prev), (z_next, z_prev)

    def x_copies(k, block):
        return both(block, q_x, k, x_send, x_recv, along_x)

    def y_copies(k, quarter):
        return both(opp_b, quarter, k, y_send, y_recv, along_y)

    def z_copies(k, quarter):
        return both(opp_b, quarter, k, z_send, z_recv, along_z)

    def cross_copies(u, over_y, over_z):
        return (
            *(remote(piece(opp_b, over_y, 2 * u, side), PIECE, dy_send.at[u, side], dy_recv.at[u, side], along_y[side]) for side in range(2)),
            *(remote(piece(opp_b, over_z, 2 * u + 1, side), PIECE, dz_send.at[u, side], dz_recv.at[u, side], along_z[side]) for side in range(2)),
        )

    quarters = (q_x, q_y, q_z, q_d)

    def mate_copy(i, u, block):
        return remote(block * ROWS + quarters[i] * QUARTER + u * UNIT, UNIT, m_send.at[i, u], m_recv.at[i, u], mate)

    def own_copy(i, block):
        return remote(block * ROWS + i * HALF, HALF, own_send.at[i], own_recv.at[i], mate)

    def sharp_copy(i, block, where):
        there = sharp_all.at[pl.ds(block * 8, 8)]
        return pltpu.make_async_remote_copy(
            src_ref=there, dst_ref=there, send_sem=sh_send.at[i], recv_sem=sh_recv.at[i],
            device_id=where, device_id_type=MESH,
        )

    for i in range(2):
        loads[i].wait()
        unit_rows(srcall, own_base + i * HALF)

    load_tgt.wait()

    def split_target(t):
        rows = tgt_raw[t * 128:(t + 1) * 128, :]
        norm = jnp.sum(rows * rows, axis=1, keepdims=True) + 1e-06
        turned = (rows / jnp.sqrt(norm)).T
        high = turned.astype(jnp.bfloat16)
        t_hi[:, t * 128:(t + 1) * 128] = high
        t_lo[:, t * 128:(t + 1) * 128] = (turned - high.astype(jnp.float32)).astype(jnp.bfloat16)

    for t in range(8):
        split_target(t)
    top_y[...] = jnp.full(top_y.shape, -1e30, jnp.float32)
    sum_y[...] = jnp.zeros(sum_y.shape, jnp.float32)
    eye = lax.broadcasted_iota(jnp.int32, (128, 128), 0) == lax.broadcasted_iota(jnp.int32, (128, 128), 1)

    def unit_of(j, i):
        near = jnp.where(j < 2, b, mate_b) * 8 + (j % 2) * 4 + i
        whole = jnp.where(j == 4, q_x, q_d) * 2 + i % 2
        split = (q_y if i % 2 == 0 else q_z) * 2 + (j - 5)
        far = (opp_b if i < 2 else opp_mate_b) * 8 + jnp.where((j == 5) | (j == 6), split, whole)
        return jnp.where(j < 4, near, far)

    def events(i, place):
        def when(slot, act):
            if slot % 6 == place and slot >= 0:
                pl.when(i == slot // 6)(act)

        def send_x(k):
            for copy in x_copies(k, b):
                copy.start()

        def relay(k):
            for copy in x_copies(k, opp_b):
                copy.wait_recv()
            for copy in (*y_copies(k, q_x), *z_copies(k, q_x)):
                copy.start()
            if k % 2 == 1:
                mate_copy(0, k // 2, opp_b).start()

        def cross(u):
            for k in (2 * u, 2 * u + 1):
                for copy in (*y_copies(k, q_y), *z_copies(k, q_z)):
                    copy.wait_recv()
            for copy in cross_copies(u, q_z, q_y):
                copy.start()
            mate_copy(1, u, opp_b).start()
            mate_copy(2, u, opp_b).start()

        def crossed(u):
            for copy in cross_copies(u, q_d, q_d):
                copy.wait_recv()
            mate_copy(3, u, opp_b).start()

        def needed(j):
            for part, u in (((0, 0), (0, 1)), ((1, 0), (2, 0)), ((1, 1), (2, 1)), ((3, 0), (3, 1)))[j]:
                mate_copy(part, u, opp_mate_b).wait_recv()

        def mate_needed():
            for part in range(2):
                own_copy(part, mate_b).wait_recv()
            for part, block in enumerate((mate_b, opp_b, opp_mate_b)):
                sharp_copy(part, block, sharp_to[part]).wait_recv()

        for k in range(4):
            when(X_SLOT[k], lambda k=k: send_x(k))
        for k in range(4):
            when(RELAY_SLOT[k], lambda k=k: relay(k))
        for u in range(2):
            when(CROSS_SLOT[u], lambda u=u: cross(u))
            when(MATE_SLOT[u], lambda u=u: crossed(u))
        for j in range(4):
            when(ROUND_SLOT[j], lambda j=j: needed(j))
        when(6, mate_needed)

    def convert(j):
        for i in range(4):
            rows = srcall[pl.ds(pl.multiple_of(unit_of(j, i) * UNIT, UNIT), UNIT), :]
            high = rows.astype(jnp.bfloat16)
            s_hi[i * UNIT:(i + 1) * UNIT, :] = high
            s_lo[i * UNIT:(i + 1) * UNIT, :] = (rows - high.astype(jnp.float32)).astype(jnp.bfloat16)

    def peaks(j, held):
        scale = tsharp_ref[...] * LOG2E
        old = top_y[...]
        new = jnp.maximum(old, scale * jnp.max(held[...], axis=0, keepdims=True))
        sum_y[...] = sum_y[...] * jnp.exp2(old - new)
        top_y[...] = new
        for i in range(4):
            here = slice(i * UNIT, (i + 1) * UNIT)
            row = jnp.broadcast_to(sharp_all[unit_of(j, i)] * LOG2E, (128, 128))
            column = jnp.sum(jnp.where(eye, row, 0.0), axis=1, keepdims=True)
            scale_x[here, :] = column
            peak_x[here, :] = jnp.max(held[here, :] * column, axis=1, keepdims=True)

    def target_sums(j, held):
        scale = tsharp_ref[...] * LOG2E
        sum_y[...] += jnp.sum(jnp.exp2(held[...] * scale - top_y[...]), axis=0, keepdims=True)

    def keep(j, held):
        for i in range(4):
            at_unit = pl.ds(pl.multiple_of(unit_of(j, i) * UNIT, UNIT), UNIT)
            for part in range(8):
                cos[part, at_unit, :] = held[i * UNIT:(i + 1) * UNIT, part * 128:(part + 1) * 128]

    def source_sums(j, held):
        for i in range(4):
            here = slice(i * UNIT, (i + 1) * UNIT)
            peak = peak_x[here, :]
            mass = jnp.sum(jnp.exp2(held[here, :] * scale_x[here, :] - peak), axis=1, keepdims=True)
            total = jnp.broadcast_to(peak + log2(mass), (128, 128))
            lse[unit_of(j, i)] = jnp.sum(jnp.where(eye, total, 0.0), axis=0, keepdims=True)

    def dot(left, right):
        return jnp.dot(left[...], right[...], preferred_element_type=jnp.float32)

    def pair_step(i, _):
        for half, (now, before) in enumerate(((buf_a, buf_b), (buf_b, buf_a))):
            j = 2 * i + half
            last = jnp.maximum(j - 1, 0)
            events(i, 3 * half)
            convert(j)
            now[...] = dot(s_hi, t_hi)
            peaks(last, before)
            events(i, 3 * half + 1)
            now[...] += dot(s_hi, t_lo)
            target_sums(last, before)
            keep(last, before)
            events(i, 3 * half + 2)
            now[...] += dot(s_lo, t_hi)
            source_sums(last, before)
            if half == 0:
                @pl.when(i == 0)
                def _():
                    top_y[...] = jnp.full(top_y.shape, -1e30, jnp.float32)
                    sum_y[...] = jnp.zeros(sum_y.shape, jnp.float32)
        return 0

    buf_b[...] = jnp.zeros(buf_b.shape, jnp.float32)
    pl.semaphore_wait(barrier, 31)
    for copy in x_copies(0, b):
        copy.start()
    sharp_all[pl.ds(b * 8, 8)] = sharp_in[...]
    sharp_to = ((mate_b, w), (opp_b, w), (opp_mate_b, w))
    for i, where in enumerate(sharp_to):
        sharp_copy(i, b, where).start()
    own_copy(0, b).start()
    own_copy(1, b).start()
    lax.fori_loop(0, 4, pair_step, 0)
    peaks(7, buf_b)
    source_sums(7, buf_b)

    def to_a(d):
        owner = (me_a + d) % 16
        return pltpu.make_async_remote_copy(
            src_ref=lse.at[pl.ds(owner * 2, 2)], dst_ref=part_a.at[d - 1], send_sem=a_send, recv_sem=a_recv,
            device_id=peer_a(d), device_id_type=MESH,
        )

    def start_a(d, _):
        to_a(d).start()
        return 0

    lax.fori_loop(1, 16, start_a, 0)
    target_sums(7, buf_b)
    keep(7, buf_b)

    def pick(t):
        def body(i, _):
            for u in range(16):
                slot = i * 16 + u
                picked[pl.ds(slot, 1), :] = cos[t, pl.ds(cand_smem[t, slot], 1), :]
            return 0

        lax.fori_loop(0, 8, body, 0)
        want = lax.broadcasted_iota(jnp.int32, (128, 128), 0) == ctgt_ref[t:t + 1, :]
        pair8[t:t + 1, :] = jnp.sum(jnp.where(want, picked[...].T, 0.0), axis=0, keepdims=True)

    for t in range(4):
        pick(t)
    pltpu.make_async_copy(part_a, part_a, a_recv).wait()
    mine = lse[pl.ds(me_a * 2, 2)]
    part_b[0] = combine(jnp.concatenate([part_a[...], mine[None]], axis=0))

    def start_b(d, _):
        pltpu.make_async_remote_copy(
            src_ref=part_b.at[0], dst_ref=part_b.at[d], send_sem=b_send, recv_sem=b_recv,
            device_id=peer_b(d), device_id_type=MESH,
        ).start()
        return 0

    lax.fori_loop(1, 16, start_b, 0)
    for t in range(4, 8):
        pick(t)
    scale_y = tsharp_ref[...]
    bwd = (top_y[...] + log2(sum_y[...]) - 4.0) * LN2 / scale_y
    for t in range(8):
        bwd8[t:t + 1, :] = bwd[:, t * 128:(t + 1) * 128]
    pltpu.make_async_copy(part_b.at[pl.ds(1, 15)], part_b.at[pl.ds(1, 15)], b_recv).wait()
    fwd_all[me_a] = (combine(part_b[...]) - 4.0) * LN2 / sharp_all[pl.ds(me_a * 2, 2)]

    def start_c(d, _):
        there = fwd_all.at[me_a]
        pltpu.make_async_remote_copy(
            src_ref=there, dst_ref=there, send_sem=c_send, recv_sem=c_recv,
            device_id=peer_a(d), device_id_type=MESH,
        ).start()
        return 0

    lax.fori_loop(1, 16, start_c, 0)

    for k in range(4):
        for copy in (*x_copies(k, b), *y_copies(k, q_x), *z_copies(k, q_x)):
            copy.wait_send()
    for u in range(2):
        for copy in cross_copies(u, q_z, q_y):
            copy.wait_send()
        for i in range(4):
            mate_copy(i, u, opp_b).wait_send()
    for i in range(2):
        own_copy(i, b).wait_send()
    for i, where in enumerate(sharp_to):
        sharp_copy(i, b, where).wait_send()
    pltpu.make_async_copy(part_a, part_a, a_send).wait()
    pltpu.make_async_copy(part_b.at[pl.ds(1, 15)], part_b.at[pl.ds(1, 15)], b_send).wait()

    def lookup(table, index):
        return jnp.take_along_axis(table, index, axis=1, mode="promise_in_bounds")

    bwd_cand = lookup(bwd8[...], ctgt_ref[...])
    sources = cand_ref[...]
    low, high = sources % 128, sources // 128
    counts = jnp.zeros((8, 128), jnp.int32)
    tile_id = lax.broadcasted_iota(jnp.int32, (8, 128), 0)
    for t in range(8):
        counts = jnp.where(tile_id == t, count_ref[t], counts)
    valid = lax.broadcasted_iota(jnp.int32, (8, 128), 1) < counts

    pltpu.make_async_copy(part_a, part_a, c_recv).wait()
    pltpu.make_async_copy(part_a, part_a, c_send).wait()
    fwd_cand = jnp.zeros((8, 128), jnp.float32)
    for r in range(32):
        row = jnp.broadcast_to(fwd_all[r // 2, r % 2], (8, 128))
        fwd_cand = jnp.where(high == r, lookup(row, low), fwd_cand)
    denom = jnp.maximum(0.5 * (fwd_cand + bwd_cand), 0.5)
    out_ref[...] = jnp.where(valid, pair8[...] / denom, 0.0)


def per_device(src_emb, src_sharp, tgt_emb, tgt_sharp, cand_src, cand_tgt, cand_count):
    vmem = pl.BlockSpec(memory_space=pltpu.VMEM)
    smem = pl.BlockSpec(memory_space=pltpu.SMEM)
    hbm = pl.BlockSpec(memory_space=pl.ANY)
    dma = pltpu.SemaphoreType.DMA
    f32, bf16 = jnp.float32, jnp.bfloat16
    return pl.pallas_call(
        kernel,
        out_shape=jax.ShapeDtypeStruct((8, 128), f32),
        in_specs=[hbm, vmem, hbm, vmem, smem, vmem, vmem, smem],
        out_specs=vmem,
        scratch_shapes=[
            pltpu.VMEM((4 * ROWS, D), f32),
            pltpu.VMEM((8, 4 * ROWS, 128), f32),
            pltpu.VMEM((ROWS, D), f32),
            pltpu.VMEM((D, ROWS), bf16),
            pltpu.VMEM((D, ROWS), bf16),
            pltpu.VMEM((HALF, D), bf16),
            pltpu.VMEM((HALF, D), bf16),
            pltpu.VMEM((32, 1, 128), f32),
            pltpu.VMEM((32, 1, 128), f32),
            pltpu.VMEM((15, 2, 1, 128), f32),
            pltpu.VMEM((16, 2, 1, 128), f32),
            pltpu.VMEM((16, 2, 1, 128), f32),
            pltpu.VMEM((HALF, ROWS), f32),
            pltpu.VMEM((HALF, ROWS), f32),
            pltpu.VMEM((HALF, 1), f32),
            pltpu.VMEM((HALF, 1), f32),
            pltpu.VMEM((1, ROWS), f32),
            pltpu.VMEM((1, ROWS), f32),
            pltpu.VMEM((8, 128), f32),
            pltpu.VMEM((128, 128), f32),
            pltpu.VMEM((8, 128), f32),
            dma((3,)), dma((2,)), dma((2,)), *[dma((4, 2))] * 6,
            *[dma((2, 2))] * 4, dma((4, 2)), dma((4, 2)), dma((3,)), dma((3,)),
            dma, dma, dma, dma, dma, dma,
        ],
        compiler_params=pltpu.CompilerParams(
            collective_id=0, has_side_effects=True, vmem_limit_bytes=60 * 1024 * 1024
        ),
        cost_estimate=pl.CostEstimate(flops=6 * 4096 * 1024 * 1024, bytes_accessed=8 << 20, transcendentals=8 << 20),
    )(
        src_emb, src_sharp.reshape(8, 1, 128), tgt_emb, tgt_sharp.reshape(1, ROWS),
        cand_src, cand_src, cand_tgt, cand_count,
    )


def solution(mesh):
    placed = (
        P("blk", None),
        P("blk"),
        P(("blk", "wide"), None),
        P(("blk", "wide")),
        P(("blk", "wide"), None),
        P(("blk", "wide"), None),
        P(("blk", "wide")),
    )
    return jax.shard_map(
        per_device, mesh=mesh, in_specs=placed, out_specs=P(("blk", "wide"), None), check_vma=False
    )
```

```python
import jax
import jax.numpy as jnp
from jax import lax
from jax.experimental import pallas as pl
from jax.experimental.pallas import tpu as pltpu
from jax.sharding import PartitionSpec as P

LOG2E = 1.4426950408889634
LN2 = 0.6931471805599453
MESH = pl.DeviceIdType.MESH
D = 1024
ROWS = 1024
UNIT = 128
HALF = 512
QUARTER = 256
PIECE = 32
GROUPS = 1
GROUP = ROWS // GROUPS
X_SLOT = (-1, 2, 4, 5, 7, 9)
RELAY_SLOT = (5, 7, 9, 10)
CROSS_SLOT = 12
MATE_SLOT = (14, 15, 17)
ROUND_SLOT = (12, 15, 18, 21)


def log2(v):
    return jnp.log(v) * LOG2E


def combine(parts):
    top = jnp.max(parts, axis=0)
    return top + log2(jnp.sum(jnp.exp2(parts - top[None]), axis=0))


def kernel(
    src_hbm, sharp_in, tgt_hbm, tsharp_ref, cand_smem, cand_ref, ctgt_ref, count_ref, out_ref,
    srcall, cos, tgt_raw, t_hi, t_lo, s_hi, s_lo, sharp_all, lse, part_a, part_b, fwd_all,
    buf_a, buf_b, scale_x, peak_x, top_y, sum_y, bwd8, picked, pair8,
    load_sem, own_send, own_recv, x_send, x_recv, y_send, y_recv, z_send, z_recv,
    dy_send, dy_recv, dz_send, dz_recv, m_send, m_recv,
    sh_send, sh_recv, a_send, a_recv, b_send, b_recv, c_send, c_recv,
):
    b = lax.axis_index("blk")
    w = lax.axis_index("wide")
    x_lo, core = b // 2, b % 2
    y, x_hi, z = w // 16, (w // 8) % 2, w % 8
    x = x_hi * 2 + x_lo
    row_q, col_q = y % 2, z % 2
    q_x = row_q * 2 + col_q
    q_y = (1 - row_q) * 2 + col_q
    q_z = row_q * 2 + 1 - col_q
    q_d = (1 - row_q) * 2 + 1 - col_q
    opp = 1 - x_lo
    mate_b = x_lo * 2 + 1 - core
    opp_b = opp * 2 + core
    opp_mate_b = opp * 2 + 1 - core

    def at(xx, yy, zz):
        return ((xx % 2) * 2 + core, yy * 16 + (xx // 2) * 8 + zz)

    x_next, x_prev = at((x + 1) % 4, y, z), at((x + 3) % 4, y, z)
    y_next, y_prev = at(x, (y + 1) % 4, z), at(x, (y + 3) % 4, z)
    z_next, z_prev = at(x, y, (z + 1) % 8), at(x, y, (z + 7) % 8)
    mate = (mate_b, w)
    me_a = core * 8 + z
    me_b = x_lo * 8 + w // 8

    def peer_a(d):
        a = (me_a + d) % 16
        return (x_lo * 2 + a // 8, (w // 8) * 8 + a % 8)

    def peer_b(d):
        g = (me_b + d) % 16
        return ((g // 8) * 2 + core, (g % 8) * 8 + z)

    own_base = b * ROWS

    def load_src(i):
        return pltpu.make_async_copy(
            src_hbm.at[pl.ds(i * HALF, HALF)],
            srcall.at[pl.ds(pl.multiple_of(own_base + i * HALF, HALF), HALF)],
            load_sem.at[i],
        )

    loads = [load_src(0), load_src(1)]
    load_tgt = pltpu.make_async_copy(tgt_hbm, tgt_raw, load_sem.at[2])
    for load in loads:
        load.start()
    load_tgt.start()

    barrier = pltpu.get_barrier_semaphore()

    def greet(d, _):
        pl.semaphore_signal(barrier, inc=1, device_id=peer_a(d), device_id_type=MESH)
        pl.semaphore_signal(barrier, inc=1, device_id=peer_b(d), device_id_type=MESH)
        return 0

    lax.fori_loop(1, 16, greet, 0)
    pl.semaphore_signal(barrier, inc=1, device_id=(opp_mate_b, w), device_id_type=MESH)

    def unit_rows(ref, start):
        def body(i, _):
            at_rows = pl.ds(pl.multiple_of(start + i * 128, 128), 128)
            rows = ref[at_rows, :]
            norm = jnp.sum(rows * rows, axis=1, keepdims=True) + 1e-06
            ref[at_rows, :] = rows * (1.0 / jnp.sqrt(norm))
            return 0

        lax.fori_loop(0, HALF // 128, body, 0)

    def remote(rows, count, send, recv, where):
        there = srcall.at[pl.ds(pl.multiple_of(rows, PIECE), count)]
        return pltpu.make_async_remote_copy(
            src_ref=there, dst_ref=there, send_sem=send, recv_sem=recv,
            device_id=where, device_id_type=MESH,
        )

    def piece(block, quarter, k, side):
        return block * ROWS + quarter * QUARTER + (k // 2) * UNIT + side * 64 + (k % 2) * PIECE

    def both(block, quarter, k, send, recv, where):
        return tuple(
            remote(piece(block, quarter, k, side), PIECE, send.at[k, side], recv.at[k, side], where[side])
            for side in range(2)
        )

    along_x, along_y, along_z = (x_next, x_prev), (y_next, y_prev), (z_next, z_prev)

    def x_copies(k, block):
        quarter, at_k = (q_x, k) if k < 4 else (q_d, k - 2)
        return tuple(
            remote(piece(block, quarter, at_k, side), PIECE, x_send.at[k, side], x_recv.at[k, side], along_x[side])
            for side in range(2)
        )

    def y_copies(k, quarter):
        return both(opp_b, quarter, k, y_send, y_recv, along_y)

    def z_copies(k, quarter):
        return both(opp_b, quarter, k, z_send, z_recv, along_z)

    def cross_copies(over_y, over_z):
        return (
            *(remote(piece(opp_b, over_y, 0, side), PIECE, dy_send.at[side], dy_recv.at[side], along_y[side]) for side in range(2)),
            *(remote(piece(opp_b, over_z, 1, side), PIECE, dz_send.at[side], dz_recv.at[side], along_z[side]) for side in range(2)),
        )

    quarters = (q_x, q_y, q_z, q_d)

    def mate_copy(i, u, block):
        return remote(block * ROWS + quarters[i] * QUARTER + u * UNIT, UNIT, m_send.at[i, u], m_recv.at[i, u], mate)

    def own_copy(i, block):
        return remote(block * ROWS + i * HALF, HALF, own_send.at[i], own_recv.at[i], mate)

    def sharp_copy(i, block, where):
        there = sharp_all.at[pl.ds(block * 8, 8)]
        return pltpu.make_async_remote_copy(
            src_ref=there, dst_ref=there, send_sem=sh_send.at[i], recv_sem=sh_recv.at[i],
            device_id=where, device_id_type=MESH,
        )

    for i in range(2):
        loads[i].wait()
        unit_rows(srcall, own_base + i * HALF)

    load_tgt.wait()

    def split_target(t):
        rows = tgt_raw[t * 128:(t + 1) * 128, :]
        norm = jnp.sum(rows * rows, axis=1, keepdims=True) + 1e-06
        turned = (rows * (1.0 / jnp.sqrt(norm))).T
        high = turned.astype(jnp.bfloat16)
        t_hi[:, t * 128:(t + 1) * 128] = high
        t_lo[:, t * 128:(t + 1) * 128] = (turned - high.astype(jnp.float32)).astype(jnp.bfloat16)

    for t in range(8):
        split_target(t)
    top_y[...] = jnp.full(top_y.shape, -1e30, jnp.float32)
    sum_y[...] = jnp.zeros(sum_y.shape, jnp.float32)
    eye = lax.broadcasted_iota(jnp.int32, (128, 128), 0) == lax.broadcasted_iota(jnp.int32, (128, 128), 1)

    def unit_of(j, i):
        near = jnp.where(j < 2, b, mate_b) * 8 + (j % 2) * 4 + i
        whole = jnp.where(j == 4, q_x, q_d) * 2 + i % 2
        split = (q_y if i % 2 == 0 else q_z) * 2 + (j - 5)
        far = (opp_b if i < 2 else opp_mate_b) * 8 + jnp.where((j == 5) | (j == 6), split, whole)
        return jnp.where(j < 4, near, far)

    def events(i, place):
        def when(slot, act):
            if slot % 6 == place and slot >= 0:
                pl.when(i == slot // 6)(act)

        def send_x(k):
            for copy in x_copies(k, b):
                copy.start()

        def relay(k):
            for copy in x_copies(k, opp_b):
                copy.wait_recv()
            for copy in (*y_copies(k, q_x), *z_copies(k, q_x)):
                copy.start()
            if k % 2 == 1:
                mate_copy(0, k // 2, opp_b).start()

        def arrived(u):
            for k in (2 * u, 2 * u + 1):
                for copy in (*y_copies(k, q_y), *z_copies(k, q_z)):
                    copy.wait_recv()

        def to_mate(u):
            mate_copy(1, u, opp_b).start()
            mate_copy(2, u, opp_b).start()

        def cross():
            arrived(0)
            for copy in cross_copies(q_z, q_y):
                copy.start()
            to_mate(0)

        def direct():
            for k in (4, 5):
                for copy in x_copies(k, opp_b):
                    copy.wait_recv()
            mate_copy(3, 1, opp_b).start()

        def last_relayed():
            arrived(1)
            to_mate(1)

        def crossed():
            for copy in cross_copies(q_d, q_d):
                copy.wait_recv()
            mate_copy(3, 0, opp_b).start()

        def needed(j):
            for part, u in (((0, 0), (0, 1)), ((1, 0), (2, 0)), ((1, 1), (2, 1)), ((3, 0), (3, 1)))[j]:
                mate_copy(part, u, opp_mate_b).wait_recv()

        def mate_needed():
            for part in range(2):
                own_copy(part, mate_b).wait_recv()
            for part, block in enumerate((mate_b, opp_b, opp_mate_b)):
                sharp_copy(part, block, sharp_to[part]).wait_recv()

        for k in range(6):
            when(X_SLOT[k], lambda k=k: send_x(k))
        for k in range(4):
            when(RELAY_SLOT[k], lambda k=k: relay(k))
        when(CROSS_SLOT, cross)
        for slot, act in zip(MATE_SLOT, (direct, last_relayed, crossed)):
            when(slot, act)
        for j in range(4):
            when(ROUND_SLOT[j], lambda j=j: needed(j))
        when(6, mate_needed)

    def convert(j):
        for i in range(4):
            rows = srcall[pl.ds(pl.multiple_of(unit_of(j, i) * UNIT, UNIT), UNIT), :]
            high = rows.astype(jnp.bfloat16)
            s_hi[i * UNIT:(i + 1) * UNIT, :] = high
            s_lo[i * UNIT:(i + 1) * UNIT, :] = (rows - high.astype(jnp.float32)).astype(jnp.bfloat16)

    def target_peaks(held, cols):
        scale = tsharp_ref[:, cols] * LOG2E
        old = top_y[:, cols]
        new = jnp.maximum(old, scale * jnp.max(held[:, cols], axis=0, keepdims=True))
        sum_y[:, cols] = sum_y[:, cols] * jnp.exp2(old - new)
        top_y[:, cols] = new

    def source_peaks(j, held, i):
        here = slice(i * UNIT, (i + 1) * UNIT)
        row = jnp.broadcast_to(sharp_all[unit_of(j, i)] * LOG2E, (128, 128))
        column = jnp.sum(jnp.where(eye, row, 0.0), axis=1, keepdims=True)
        scale_x[here, :] = column
        peak_x[here, :] = jnp.max(held[here, :] * column, axis=1, keepdims=True)

    def target_sums(held, cols):
        scale = tsharp_ref[:, cols] * LOG2E
        sum_y[:, cols] += jnp.sum(jnp.exp2(held[:, cols] * scale - top_y[:, cols]), axis=0, keepdims=True)

    def keep(j, held, i):
        at_unit = pl.ds(pl.multiple_of(unit_of(j, i) * UNIT, UNIT), UNIT)
        for part in range(8):
            cos[part, at_unit, :] = held[i * UNIT:(i + 1) * UNIT, part * 128:(part + 1) * 128]

    def source_sums(j, held, i):
        here = slice(i * UNIT, (i + 1) * UNIT)
        peak = peak_x[here, :]
        mass = jnp.sum(jnp.exp2(held[here, :] * scale_x[here, :] - peak), axis=1, keepdims=True)
        total = jnp.broadcast_to(peak + log2(mass), (128, 128))
        lse[unit_of(j, i)] = jnp.sum(jnp.where(eye, total, 0.0), axis=0, keepdims=True)

    def dot(left, right, cols):
        return jnp.dot(left[...], right[:, cols], preferred_element_type=jnp.float32)

    def pair_step(i, _):
        for half, (now, before) in enumerate(((buf_a, buf_b), (buf_b, buf_a))):
            j = 2 * i + half
            last = jnp.maximum(j - 1, 0)
            events(i, 3 * half)
            convert(j)
            for g in range(GROUPS):
                cols = slice(g * GROUP, (g + 1) * GROUP)
                now[:, cols] = dot(s_hi, t_hi, cols)
                target_peaks(before, cols)
                for part in range(g * 4 // GROUPS, (g + 1) * 4 // GROUPS):
                    source_peaks(last, before, part)
            events(i, 3 * half + 1)
            for g in range(GROUPS):
                cols = slice(g * GROUP, (g + 1) * GROUP)
                now[:, cols] += dot(s_hi, t_lo, cols)
                target_sums(before, cols)
                for part in range(g * 4 // GROUPS, (g + 1) * 4 // GROUPS):
                    keep(last, before, part)
            events(i, 3 * half + 2)
            for g in range(GROUPS):
                cols = slice(g * GROUP, (g + 1) * GROUP)
                now[:, cols] += dot(s_lo, t_hi, cols)
                for part in range(g * 4 // GROUPS, (g + 1) * 4 // GROUPS):
                    source_sums(last, before, part)
            if half == 0:
                @pl.when(i == 0)
                def _():
                    top_y[...] = jnp.full(top_y.shape, -1e30, jnp.float32)
                    sum_y[...] = jnp.zeros(sum_y.shape, jnp.float32)
        return 0

    buf_b[...] = jnp.zeros(buf_b.shape, jnp.float32)
    pl.semaphore_wait(barrier, 31)
    for copy in x_copies(0, b):
        copy.start()
    sharp_all[pl.ds(b * 8, 8)] = sharp_in[...]
    sharp_to = ((mate_b, w), (opp_b, w), (opp_mate_b, w))
    for i, where in enumerate(sharp_to):
        sharp_copy(i, b, where).start()
    own_copy(0, b).start()
    own_copy(1, b).start()
    lax.fori_loop(0, 4, pair_step, 0)
    for part in range(4):
        source_peaks(7, buf_b, part)
        source_sums(7, buf_b, part)

    def to_a(d):
        owner = (me_a + d) % 16
        return pltpu.make_async_remote_copy(
            src_ref=lse.at[pl.ds(owner * 2, 2)], dst_ref=part_a.at[d - 1], send_sem=a_send, recv_sem=a_recv,
            device_id=peer_a(d), device_id_type=MESH,
        )

    def start_a(d, _):
        to_a(d).start()
        return 0

    lax.fori_loop(1, 16, start_a, 0)
    target_peaks(buf_b, slice(0, ROWS))
    target_sums(buf_b, slice(0, ROWS))
    for part in range(4):
        keep(7, buf_b, part)

    def pick(t):
        def body(i, _):
            for u in range(16):
                slot = i * 16 + u
                picked[pl.ds(slot, 1), :] = cos[t, pl.ds(cand_smem[t, slot], 1), :]
            return 0

        lax.fori_loop(0, 8, body, 0)
        want = lax.broadcasted_iota(jnp.int32, (128, 128), 0) == ctgt_ref[t:t + 1, :]
        pair8[t:t + 1, :] = jnp.sum(jnp.where(want, picked[...].T, 0.0), axis=0, keepdims=True)

    for t in range(4):
        pick(t)
    pltpu.make_async_copy(part_a, part_a, a_recv).wait()
    mine = lse[pl.ds(me_a * 2, 2)]
    part_b[0] = combine(jnp.concatenate([part_a[...], mine[None]], axis=0))

    def start_b(d, _):
        pltpu.make_async_remote_copy(
            src_ref=part_b.at[0], dst_ref=part_b.at[d], send_sem=b_send, recv_sem=b_recv,
            device_id=peer_b(d), device_id_type=MESH,
        ).start()
        return 0

    lax.fori_loop(1, 16, start_b, 0)
    for t in range(4, 8):
        pick(t)
    scale_y = tsharp_ref[...]
    bwd = (top_y[...] + log2(sum_y[...]) - 4.0) * LN2 / scale_y
    for t in range(8):
        bwd8[t:t + 1, :] = bwd[:, t * 128:(t + 1) * 128]
    pltpu.make_async_copy(part_b.at[pl.ds(1, 15)], part_b.at[pl.ds(1, 15)], b_recv).wait()
    fwd_all[me_a] = (combine(part_b[...]) - 4.0) * LN2 / sharp_all[pl.ds(me_a * 2, 2)]

    def start_c(d, _):
        there = fwd_all.at[me_a]
        pltpu.make_async_remote_copy(
            src_ref=there, dst_ref=there, send_sem=c_send, recv_sem=c_recv,
            device_id=peer_a(d), device_id_type=MESH,
        ).start()
        return 0

    lax.fori_loop(1, 16, start_c, 0)

    for k in range(6):
        for copy in x_copies(k, b):
            copy.wait_send()
    for k in range(4):
        for copy in (*y_copies(k, q_x), *z_copies(k, q_x)):
            copy.wait_send()
    for copy in cross_copies(q_z, q_y):
        copy.wait_send()
    for i in range(4):
        for u in range(2):
            mate_copy(i, u, opp_b).wait_send()
    for i in range(2):
        own_copy(i, b).wait_send()
    for i, where in enumerate(sharp_to):
        sharp_copy(i, b, where).wait_send()
    pltpu.make_async_copy(part_a, part_a, a_send).wait()
    pltpu.make_async_copy(part_b.at[pl.ds(1, 15)], part_b.at[pl.ds(1, 15)], b_send).wait()

    def lookup(table, index):
        return jnp.take_along_axis(table, index, axis=1, mode="promise_in_bounds")

    bwd_cand = lookup(bwd8[...], ctgt_ref[...])
    sources = cand_ref[...]
    low, high = sources % 128, sources // 128
    counts = jnp.zeros((8, 128), jnp.int32)
    tile_id = lax.broadcasted_iota(jnp.int32, (8, 128), 0)
    for t in range(8):
        counts = jnp.where(tile_id == t, count_ref[t], counts)
    valid = lax.broadcasted_iota(jnp.int32, (8, 128), 1) < counts

    pltpu.make_async_copy(part_a, part_a, c_recv).wait()
    pltpu.make_async_copy(part_a, part_a, c_send).wait()
    fwd_cand = jnp.zeros((8, 128), jnp.float32)
    for r in range(32):
        row = jnp.broadcast_to(fwd_all[r // 2, r % 2], (8, 128))
        fwd_cand = jnp.where(high == r, lookup(row, low), fwd_cand)
    denom = jnp.maximum(0.5 * (fwd_cand + bwd_cand), 0.5)
    out_ref[...] = jnp.where(valid, pair8[...] / denom, 0.0)


def per_device(src_emb, src_sharp, tgt_emb, tgt_sharp, cand_src, cand_tgt, cand_count):
    vmem = pl.BlockSpec(memory_space=pltpu.VMEM)
    smem = pl.BlockSpec(memory_space=pltpu.SMEM)
    hbm = pl.BlockSpec(memory_space=pl.ANY)
    dma = pltpu.SemaphoreType.DMA
    f32, bf16 = jnp.float32, jnp.bfloat16
    return pl.pallas_call(
        kernel,
        out_shape=jax.ShapeDtypeStruct((8, 128), f32),
        in_specs=[hbm, vmem, hbm, vmem, smem, vmem, vmem, smem],
        out_specs=vmem,
        scratch_shapes=[
            pltpu.VMEM((4 * ROWS, D), f32),
            pltpu.VMEM((8, 4 * ROWS, 128), f32),
            pltpu.VMEM((ROWS, D), f32),
            pltpu.VMEM((D, ROWS), bf16),
            pltpu.VMEM((D, ROWS), bf16),
            pltpu.VMEM((HALF, D), bf16),
            pltpu.VMEM((HALF, D), bf16),
            pltpu.VMEM((32, 1, 128), f32),
            pltpu.VMEM((32, 1, 128), f32),
            pltpu.VMEM((15, 2, 1, 128), f32),
            pltpu.VMEM((16, 2, 1, 128), f32),
            pltpu.VMEM((16, 2, 1, 128), f32),
            pltpu.VMEM((HALF, ROWS), f32),
            pltpu.VMEM((HALF, ROWS), f32),
            pltpu.VMEM((HALF, 1), f32),
            pltpu.VMEM((HALF, 1), f32),
            pltpu.VMEM((1, ROWS), f32),
            pltpu.VMEM((1, ROWS), f32),
            pltpu.VMEM((8, 128), f32),
            pltpu.VMEM((128, 128), f32),
            pltpu.VMEM((8, 128), f32),
            dma((3,)), dma((2,)), dma((2,)), dma((6, 2)), dma((6, 2)), *[dma((4, 2))] * 4,
            *[dma((2,))] * 4, dma((4, 2)), dma((4, 2)), dma((3,)), dma((3,)),
            dma, dma, dma, dma, dma, dma,
        ],
        compiler_params=pltpu.CompilerParams(
            collective_id=0, has_side_effects=True, vmem_limit_bytes=60 * 1024 * 1024
        ),
        cost_estimate=pl.CostEstimate(flops=6 * 4096 * 1024 * 1024, bytes_accessed=8 << 20, transcendentals=8 << 20),
    )(
        src_emb, src_sharp.reshape(8, 1, 128), tgt_emb, tgt_sharp.reshape(1, ROWS),
        cand_src, cand_src, cand_tgt, cand_count,
    )


def solution(mesh):
    placed = (
        P("blk", None),
        P("blk"),
        P(("blk", "wide"), None),
        P(("blk", "wide")),
        P(("blk", "wide"), None),
        P(("blk", "wide"), None),
        P(("blk", "wide")),
    )
    return jax.shard_map(
        per_device, mesh=mesh, in_specs=placed, out_specs=P(("blk", "wide"), None), check_vma=False
    )
```
